32 devices in a mesh: groups: 2 (over y), vox: 4 (over z), freq: 2 (over x), sub: 2 (over core).
Axes of the slice: x: 2, y: 2, z: 4, core: 2. Of those that a mesh axis runs over, the one named last changes fastest.
Arguments:
- residual: bfloat16 [4, 1024, 1024], P(('groups', 'freq'), 'vox', 'sub'), parts along dimension 0, may hold values from -6 to 6
- green: bfloat16 [4, 1024, 8192], P(('groups', 'freq'), None, 'vox'), parts along dimension 0, may hold values from -0.15625 to 0.15625
- active: int32 [4, 1024], P(('groups', 'freq')), parts along dimension 0, may hold values 0 or 1
- aperture: int32 [4], P(('groups', 'freq')), parts along dimension 0, may hold values from 256 to 511
- step_gain: float32 [4], P(('groups', 'freq')), parts along dimension 0, may hold values from 6 to 24
- block_region: int32 [128], P(('groups', 'vox')), parts along dimension 0, may hold values from 0 to 15
- strength: float32 [16], replicated, may hold values from 0.1 to 1
Outputs:
- updated: float32 [4, 1024, 1024], P(('groups', 'freq'), 'vox', 'sub'), parts along dimension 0
The draws below stay inside these ranges and needn't reach their ends.
There are 2 independent parts, one for each index of `groups`. The reference program is written for one: setup_inputs(seed, part) draws one part's arguments, and reference() takes and returns one part's arrays. A program takes and returns all parts, laid end to end along the dimension named above; an argument that names none is the same for every part. Nothing has to cross between parts.
All inputs are finite; a program needn't handle non-finite values. No bound on the sum of `active` on one device may be relied on, other than what follows from the above.
Results may differ from the reference program's by a relative error of at most 0.0026.
Values may be sent and summed in bfloat16 or wider, within the bound.
No kernel may reach another device: no remote copies, remote signals or barrier semaphores. Data moves between devices by JAX's collectives and lax.ppermute only.
A program may use at most 64 MiB of HBM per device.

```python
import math
import jax
import jax.numpy as jnp
from jax import lax

NE = 1024
BLOCK = 128
REGIONS = 16
FREQS = 2
VOXELS = 8192
NBLK = 64


def place_ends(result, own_key, low, high):
    longest = result.shape.index(max(result.shape))
    spots = []
    for shift in (0, 1):
        where = [jax.random.randint(jax.random.fold_in(own_key, axis), (), 0, length) for axis, length in enumerate(result.shape)]
        where[longest] = (where[longest] + shift) % result.shape[longest]
        spots.append(tuple(where))
    return result.at[spots[0]].set(low).at[spots[1]].set(high)


def strengthened(values, rng, source, target, shards_of, factor):
    def block_of(position):
        return (jnp.arange(values.shape[position]) // (values.shape[position] // shards_of)).reshape((-1,) + (1,) * (values.ndim - 1 - position))

    one_side = jax.random.permutation(rng, shards_of)[block_of(target)]
    other_side = (block_of(target) + shards_of // 2) % shards_of
    return jnp.where((block_of(source) == one_side) | (block_of(source) == other_side), factor * values, values)


def block_levels(own_key, shape, pieces, low, largest):
    def one(dim, blocks):
        steps = jax.random.uniform(jax.random.fold_in(jax.random.fold_in(own_key, 6), dim), (blocks,), jnp.float32, low / len(pieces), largest / len(pieces))
        return jnp.repeat(jnp.exp(steps), shape[dim] // blocks).reshape((-1,) + (1,) * (len(shape) - dim - 1))

    loudness = one(*pieces[0])
    for cut in pieces[1:]:
        loudness = loudness * one(*cut)
    return loudness


def normal_values(key, extent, width, bound, split=(), kind=jnp.bfloat16):
    drawn = jax.random.normal(key, extent, jnp.float32) * width
    if len(split) > 0:
        drawn = block_levels(key, extent, split, -0.22, 0.18) * drawn
    return jnp.clip(drawn, min=-bound, max=bound).astype(kind)


def heavy_noise(stream_key, extent, scale, most, cuts, heavy, kind=jnp.bfloat16):
    array = scale * jax.random.normal(stream_key, extent, jnp.float32)
    if cuts:
        array = array * block_levels(stream_key, extent, cuts, -0.22, 0.18)
    return jnp.clip(strengthened(array, jax.random.fold_in(stream_key, 3), *heavy), -most, most).astype(kind)


def setup_inputs(seed: int = 0, part: int = 0) -> dict:
    arg_keys = jax.random.split(jax.random.key(seed), 8)
    own_keys = jax.random.split(jax.random.fold_in(arg_keys[7], part), 8)
    return {
        "residual": normal_values(own_keys[0], (FREQS, NE, NE), 1.0, 6.0, ((0, 2), (1, 4), (2, 2))),
        "green": heavy_noise(own_keys[1], (FREQS, NE, VOXELS), (3 * NE) ** -0.5, 0.15625, ((0, 2), (2, 4)), (2, 1, 4, 2.0)),
        "active": place_ends((jax.random.randint(own_keys[2], (FREQS, NE), 0, 8) < 7).astype(jnp.int32), jax.random.fold_in(own_keys[2], 1), 0, 1),
        "aperture": jax.random.randint(own_keys[3], (FREQS,), NE // 4, NE // 2).astype(jnp.int32),
        "step_gain": jnp.clip(jnp.exp(math.log(24.0) - 1.3862944 * jax.random.uniform(own_keys[4], (FREQS,), jnp.float32) ** block_levels(own_keys[4], (FREQS,), ((0, 2),), -0.2, 0.2)), 6.0, 24.0),
        "block_region": place_ends(jax.random.randint(own_keys[5], (NBLK,), 0, REGIONS), jax.random.fold_in(own_keys[5], 1), 0, REGIONS - 1).astype(jnp.int32),
        "strength": jnp.clip(jnp.exp(jax.random.uniform(arg_keys[6], (REGIONS,), jnp.float32, math.log(0.1), math.log(1.0))), 0.1, 1.0),
    }


smooth_sq = 0.0625

def build_mask(active, aperture):
    element_ids = jnp.arange(NE, dtype=jnp.int32)
    distance = jnp.abs(element_ids[:, None] - element_ids[None, :])
    in_band = (distance[None, :, :] <= aperture[:, None, None]).astype(jnp.int32)
    return active[:, :, None] * active[:, None, :] * in_band

def penalize(image_sum, strength_map):
    return image_sum - strength_map * image_sum / jnp.sqrt(image_sum * image_sum + smooth_sq)

def reference(residual, green, active, aperture, step_gain, block_region, strength):
    pair_mask = build_mask(active, aperture)
    masked = residual * pair_mask.astype(jnp.bfloat16)

    def image_one(operands):
        masked_f, green_f = operands
        beamed = jnp.dot(masked_f.T, green_f, preferred_element_type=jnp.float32)
        return lax.optimization_barrier(jnp.sum(green_f.astype(jnp.float32) * beamed, axis=0))
    image_sum = lax.optimization_barrier(jnp.sum(lax.map(image_one, (masked, green)), axis=0))
    strength_map = jnp.repeat(strength[block_region], BLOCK)
    scaled = penalize(image_sum, strength_map)

    def gradient_one(green_f):
        weighted = (green_f.astype(jnp.float32) * scaled[None, :]).astype(jnp.bfloat16)
        return jnp.dot(green_f, weighted.T, preferred_element_type=jnp.float32)
    gradient = lax.map(gradient_one, green)
    return pair_mask.astype(jnp.float32) * (residual.astype(jnp.float32) - step_gain[:, None, None] * gradient)
```

```python
import jax
import jax.numpy as jnp
from jax import lax
from jax.sharding import PartitionSpec as P

BLOCK = 128
REGIONS = 16


smooth_sq = 0.0625


def penalize(image_sum, strength_map):
    return image_sum - strength_map * image_sum / jnp.sqrt(image_sum * image_sum + smooth_sq)


def rotation(count, step):
    return [(i, (i + step) % count) for i in range(count)]


def body(sizes, residual, green, active, aperture, step_gain, block_region, strength):
    vox_n = sizes["vox"]
    local_data = residual[0]
    green_rows = green[0]
    element_on = active[0]
    rows_local = local_data.shape[0]
    cols_local = local_data.shape[1]
    me = lax.axis_index("vox")
    row_start = me * rows_local
    col_start = lax.axis_index("sub") * cols_local
    row_ids = row_start + jnp.arange(rows_local, dtype=jnp.int32)
    col_ids = col_start + jnp.arange(cols_local, dtype=jnp.int32)
    row_on = lax.dynamic_slice_in_dim(element_on, row_start, rows_local)
    col_on = lax.dynamic_slice_in_dim(element_on, col_start, cols_local)
    in_band = (jnp.abs(row_ids[:, None] - col_ids[None, :]) <= aperture[0]).astype(jnp.int32)
    pair_mask = row_on[:, None] * col_on[None, :] * in_band
    masked = local_data * pair_mask.astype(jnp.bfloat16)
    tx_green = lax.dynamic_slice_in_dim(green_rows, col_start, cols_local, 0)

    def rows_of(array, owner):
        return lax.dynamic_slice_in_dim(array, owner * rows_local, rows_local, 0)

    gathered = jnp.zeros((vox_n * rows_local, cols_local), masked.dtype)
    for step in range(vox_n):
        piece = masked if step == 0 else lax.ppermute(masked, "vox", rotation(vox_n, step))
        gathered = lax.dynamic_update_slice_in_dim(
            gathered, piece, (me - step) % vox_n * rows_local, 0
        )
    beamed = lax.dot_general(
        gathered, green_rows, (((0,), (0,)), ((), ())), preferred_element_type=jnp.float32
    )
    image_sum = jnp.sum(tx_green.astype(jnp.float32) * beamed, axis=0).reshape(-1, BLOCK)
    region_ids = jnp.arange(REGIONS, dtype=jnp.int32)
    onehot = (block_region[:, None] == region_ids[None, :]).astype(jnp.float32)
    block_strength = jnp.dot(onehot, strength, precision=lax.Precision.HIGHEST)
    for axis in ("sub", "freq"):
        count = sizes[axis]
        own = image_sum
        for step in range(1, count):
            image_sum = image_sum + lax.ppermute(own, axis, rotation(count, step))
    scaled = penalize(image_sum, block_strength[:, None]).reshape(-1)
    weighted = (tx_green.astype(jnp.float32) * scaled[None, :]).astype(jnp.bfloat16)
    gradient = lax.dot_general(
        green_rows, weighted, (((1,), (1,)), ((), ())), preferred_element_type=jnp.float32
    )
    sendable = gradient.astype(jnp.bfloat16)
    total = rows_of(gradient, me)
    for step in range(1, vox_n):
        piece = rows_of(sendable, (me + step) % vox_n)
        total = total + lax.ppermute(piece, "vox", rotation(vox_n, step)).astype(jnp.float32)
    updated = pair_mask.astype(jnp.float32) * (
        local_data.astype(jnp.float32) - step_gain[0] * total
    )
    return updated[None]


def solution(mesh):
    sizes = dict(mesh.shape)
    in_specs = (
        P(("groups", "freq"), "vox", "sub"),
        P(("groups", "freq"), None, "vox"),
        P(("groups", "freq"), None),
        P(("groups", "freq")),
        P(("groups", "freq")),
        P(("groups", "vox")),
        P(),
    )
    out_specs = P(("groups", "freq"), "vox", "sub")

    def local(*arrays):
        return body(sizes, *arrays)

    return jax.shard_map(local, mesh=mesh, in_specs=in_specs, out_specs=out_specs, check_vma=False)
```
